1024 devices in a mesh: ep: 32 (over x, y, core), dp: 32 (over z).
Axes of the slice: x: 4, y: 4, z: 32, core: 2. Of those that a mesh axis runs over, the one named last changes fastest.
Arguments:
- rows_in: bfloat16 [131072, 2048], P(('ep', 'dp')), may hold values from -3 to 3
- grads_in: bfloat16 [131072, 2048], P(('ep', 'dp')), may hold values from -3 to 3
- expert_ids: int32 [131072, 1], P(('ep', 'dp')), may hold values from 0 to 31; in each aligned block of 128 rows (0 to 127, 128 to 255, ...) at most 8 rows name the same one
- w_gate: bfloat16 [32, 2048, 640], P('ep'), may hold values from -0.125 to 0.125
- w_up: bfloat16 [32, 2048, 640], P('ep'), may hold values from -0.125 to 0.125
- w_down: bfloat16 [32, 640, 2048], P('ep'), may hold values from -0.25 to 0.25
- project: bfloat16 [32, 2, 2048, 64], P('ep'), may hold values from -0.75 to 0.75
- moment_one: float32 [32, 122880], P('ep', 'dp'), may hold values from -3 to 3
- moment_two: float32 [32, 122880], P('ep', 'dp'), may hold values from 0.01 to 0.3
Outputs:
- rows_out: bfloat16 [131072, 2048], P(('ep', 'dp'))
- first_new: float32 [32, 122880], P('ep', 'dp')
- second_new: float32 [32, 122880], P('ep', 'dp')
- step_gate: bfloat16 [32, 2048, 640], P('ep', 'dp')
- step_up: bfloat16 [32, 2048, 640], P('ep', 'dp')
- step_down: bfloat16 [32, 640, 2048], P('ep', None, 'dp')
The draws below stay inside these ranges and needn't reach their ends.
Inputs may be any that keep to these rules, and one draw needn't show every extreme that they name: `expert_ids`: within the 128 rows of one device no expert is named by more than 8 rows, and some devices name one expert by exactly 8 rows.
All inputs are finite; a program needn't handle non-finite values.
Results may differ from the reference program's by a relative error of at most 0.0049.
Values may be sent and summed in bfloat16 or wider, within the bound.
A program may use at most 64 MiB of HBM per device.

```python
import math
import jax
import jax.numpy as jnp
import numpy as np
from jax import lax

D = 2048
FF = 640
RANK = 64
ROWS_DEV = 128
EXPERTS = 32
CAP = 8
ROWS = 131072
N_EP = 32
N_DP = 32


def block_scale(stream_key, dims, split, least, top_value):
    level = 1.0
    for position, shards_of in split:
        heights = jax.random.uniform(jax.random.fold_in(jax.random.fold_in(stream_key, 6), position), (shards_of,), jnp.float32, least / len(split), top_value / len(split))
        level = level * jnp.repeat(jnp.exp(heights), dims[position] // shards_of).reshape((-1,) + (1,) * (len(dims) - 1 - position))
    return level


def deal_out(rng, own, number, rows, amount, top, reach, skew):
    order = jax.random.permutation(rng, amount)
    crowded, ordinary = portions_of(amount, rows * top, reach, skew, True), portions_of(amount, rows * top, reach, skew, False)
    places = jnp.arange(amount)

    def named(tallies, rotation):
        used = int((tallies > 0).sum())
        fixed = max(1, used // 4)
        moved = fixed + (places - fixed + rotation * (used - fixed)) % max(1, amount - fixed)
        return jnp.zeros((amount,), jnp.int32).at[order[jnp.where(places < fixed, places, moved)]].set(jnp.asarray(tallies, jnp.int32))

    tallies = jnp.where(number % 4 == 0, named(crowded, number // 4), named(ordinary, number - number // 4 - 1))
    mixed = jax.random.permutation(jax.random.fold_in(own, 3), amount)
    source_of, taker = mixed[0:amount // 2 * 2:2], mixed[1:amount // 2 * 2:2]
    slack = jnp.minimum(tallies[source_of] - 1, reach - tallies[taker]) // 2
    slack = jnp.where((source_of == order[0]) | (taker == order[0]) | (tallies[taker] == 0), 0, jnp.maximum(slack, 0))
    moved = jax.random.randint(jax.random.fold_in(own, 4), (amount // 2,), 0, 1 << 20) % (slack + 1)
    tallies = tallies.at[source_of].add(-moved).at[taker].add(moved)
    labels = jnp.searchsorted(jnp.cumsum(tallies), jnp.arange(rows * top), side="right").astype(jnp.int32)
    listing = labels.reshape(top, rows).T
    listing = listing[jax.random.permutation(jax.random.fold_in(own, 1), rows)]
    rotation = jax.random.randint(jax.random.fold_in(own, 2), (rows, 1), 0, top)
    return jnp.take_along_axis(listing, (jnp.arange(top)[None, :] + rotation) % top, axis=1)


def portions_of(amount, total, limit, slope, full):
    loads = [(1 << 20) // math.isqrt(rank ** slope) + 1 for rank in range(1, amount + 1)]
    largest = limit if full else min(limit, max(-(-total // amount), total * loads[0] // sum(loads)))
    least = 1 if total - largest >= amount - 1 else 0
    holding, spare = [largest] + [least] * (amount - 1), total - largest - least * (amount - 1)
    while spare > 0:
        movable = [i for i in range(1, amount) if holding[i] < largest] or [i for i in range(1, amount) if holding[i] < limit]
        whole, left = sum([loads[i] for i in movable]), spare
        for i in movable:
            addition = min(limit - holding[i], max(1, left * loads[i] // whole), spare)
            holding[i] = holding[i] + addition
            spare = spare - addition
    return np.array(holding)


def gaussian(key, extent, scale, most, split=(), kind=jnp.bfloat16):
    level = block_scale(key, extent, split, -0.22, 0.18) if split else 1.0
    result = jax.random.normal(key, extent, jnp.float32) * scale * level
    return jnp.minimum(jnp.maximum(result, -most), most).astype(kind)


def setup_inputs(seed: int = 0) -> dict:
    key_of = jax.random.split(jax.random.key(seed), 10)
    rows_in = gaussian(key_of[0], (ROWS, D), 0.5, 3.0, ((0, 1024),))
    grads_in = gaussian(key_of[1], (ROWS, D), 0.5, 3.0, ((0, 1024),))
    expert_ids_keys = jax.random.split(jax.random.fold_in(key_of[2], 1), ROWS // ROWS_DEV)
    expert_ids_turns = jax.random.permutation(jax.random.fold_in(key_of[2], 3), ROWS // ROWS_DEV)
    expert_ids = jax.vmap(lambda own, number: deal_out(jax.random.fold_in(key_of[2], 2), own, number, ROWS_DEV, EXPERTS, 1, CAP, 2))(expert_ids_keys, expert_ids_turns).reshape((ROWS, 1))
    w_gate = gaussian(key_of[3], (EXPERTS, D, FF), D ** -0.5, 0.125, ((0, 32),))
    w_up = gaussian(key_of[4], (EXPERTS, D, FF), D ** -0.5, 0.125, ((0, 32),))
    w_down = gaussian(key_of[5], (EXPERTS, FF, D), FF ** -0.5, 0.25, ((0, 32),))
    project = gaussian(key_of[6], (EXPERTS, 2, D, RANK), RANK ** -0.5, 0.75, ((0, 32),))
    moment_one = gaussian(key_of[7], (EXPERTS, 3 * RANK * FF), 0.3, 3.0, ((0, 32), (1, 32)), jnp.float32)
    moment_two = jnp.clip(jnp.exp(math.log(0.3) - 3.4011974 * jax.random.uniform(key_of[8], (EXPERTS, 3 * RANK * FF), jnp.float32) ** block_scale(key_of[8], (EXPERTS, 3 * RANK * FF), ((0, 32), (1, 32)), -0.2, 0.2)), 0.01, 0.3)
    return {"rows_in": rows_in, "grads_in": grads_in, "expert_ids": expert_ids, "w_gate": w_gate, "w_up": w_up, "w_down": w_down, "project": project, "moment_one": moment_one, "moment_two": moment_two}


beta_one = 0.9
beta_two = 0.999
adam_eps = 1e-08
bias_one = 1.0 - 0.9 ** 10
bias_two = 1.0 - 0.999 ** 10
highest = lax.Precision.HIGHEST

def wide_dot(left, right):
    return jnp.dot(left.astype(jnp.float32), right.astype(jnp.float32), precision=highest)

def expert_pass(rows_x, rows_g, gate_mat, up_mat, down_mat, proj_mats):
    gate_pre = wide_dot(rows_x, gate_mat)
    up_pre = wide_dot(rows_x, up_mat)
    sigmoid = jax.nn.sigmoid(gate_pre)
    hidden = (gate_pre * sigmoid * up_pre).astype(jnp.bfloat16)
    hidden_grad = wide_dot(rows_g, down_mat.T)
    up_grad = (hidden_grad * gate_pre * sigmoid).astype(jnp.bfloat16)
    gate_grad = (hidden_grad * up_pre * sigmoid * (1.0 + gate_pre * (1.0 - sigmoid))).astype(jnp.bfloat16)
    rows_grad = (wide_dot(gate_grad, gate_mat.T) + wide_dot(up_grad, up_mat.T)).astype(jnp.bfloat16)
    proj_in = wide_dot(rows_x, proj_mats[0])
    proj_down = wide_dot(rows_g, proj_mats[1])
    grad_gate = wide_dot(proj_in.T, gate_grad)
    grad_up = wide_dot(proj_in.T, up_grad)
    grad_down = wide_dot(proj_down.T, hidden)
    return (rows_grad, jnp.stack([grad_gate, grad_up, grad_down]))

def reference(rows_in, grads_in, expert_ids, w_gate, w_up, w_down, project, moment_one, moment_two):
    targets = expert_ids[:, 0].astype(jnp.int32)
    total_rows = ROWS_DEV * N_EP * N_DP
    blocks = N_EP * N_DP
    per_expert = blocks * CAP
    block_targets = targets.reshape(blocks, ROWS_DEV)
    onehot = (block_targets[:, :, None] == jnp.arange(EXPERTS, dtype=jnp.int32)[None, None, :]).astype(jnp.int32)
    ranked = lax.optimization_barrier(jnp.sum(jnp.cumsum(onehot, axis=1) * onehot, axis=2)) - 1
    block_ids = jnp.arange(blocks, dtype=jnp.int32)[:, None]
    slots = (block_ids * CAP + ranked).reshape(-1).astype(jnp.int32)
    table = jnp.full((EXPERTS, per_expert), total_rows, jnp.int32)
    table = table.at[targets, slots].set(jnp.arange(total_rows, dtype=jnp.int32))

    def one_expert(expert, state_pair):
        rows_acc, grad_all = state_pair
        picked = lax.dynamic_index_in_dim(table, expert, 0, keepdims=False)
        rows_x = jnp.take(rows_in, picked, axis=0, mode='fill', fill_value=0)
        rows_g = jnp.take(grads_in, picked, axis=0, mode='fill', fill_value=0)
        gate_one = lax.dynamic_index_in_dim(w_gate, expert, 0, keepdims=False)
        up_one = lax.dynamic_index_in_dim(w_up, expert, 0, keepdims=False)
        down_one = lax.dynamic_index_in_dim(w_down, expert, 0, keepdims=False)
        proj_one = lax.dynamic_index_in_dim(project, expert, 0, keepdims=False)
        rows_grad, grad_terms = expert_pass(rows_x, rows_g, gate_one, up_one, down_one, proj_one)
        rows_acc = rows_acc.at[picked].set(rows_grad, mode='drop')
        grad_all = lax.dynamic_update_index_in_dim(grad_all, grad_terms, expert, 0)
        return (rows_acc, grad_all)
    initial = (jnp.zeros_like(rows_in), jnp.zeros((EXPERTS, 3, RANK, FF), jnp.float32))
    rows_out, grad_all = lax.fori_loop(0, EXPERTS, one_expert, initial)
    grad_flat = grad_all.reshape(EXPERTS, 3 * RANK * FF) * (1.0 / math.sqrt(total_rows))
    first_new = beta_one * moment_one + (1.0 - beta_one) * grad_flat
    second_new = beta_two * moment_two + (1.0 - beta_two) * grad_flat * grad_flat
    update = first_new / bias_one / (jnp.sqrt(second_new / bias_two) + adam_eps)
    update = update.reshape(EXPERTS, 3, RANK, FF)
    proj_wide = project.astype(jnp.float32)
    step_gate = jnp.einsum('edr,erf->edf', proj_wide[:, 0], update[:, 0], precision=highest).astype(jnp.bfloat16)
    step_up = jnp.einsum('edr,erf->edf', proj_wide[:, 0], update[:, 1], precision=highest).astype(jnp.bfloat16)
    step_down = jnp.einsum('erf,edr->efd', update[:, 2], proj_wide[:, 1], precision=highest).astype(jnp.bfloat16)
    return (rows_out, first_new, second_new, step_gate, step_up, step_down)
```

```python
import functools
import math

import jax
import jax.numpy as jnp
from jax import lax
from jax.experimental import pallas as pl
from jax.experimental.pallas import tpu as pltpu
from jax.sharding import PartitionSpec as P

beta_one = 0.9
beta_two = 0.999
adam_eps = 1e-08
bias_one = 1.0 - 0.9**10
bias_two = 1.0 - 0.999**10

MESH = pl.DeviceIdType.MESH
CAP = 8
GROUP = 4
LANES = 128
F32 = jnp.float32
BF16 = jnp.bfloat16


def dot(a, b):
    return jnp.dot(a, b, preferred_element_type=F32)


def dot_nt(a, b):
    return lax.dot_general(a, b, (((1,), (1,)), ((), ())), preferred_element_type=F32)


def dot_tn(a, b):
    return lax.dot_general(a, b, (((0,), (0,)), ((), ())), preferred_element_type=F32)


def remote(src, dst, send_sem, recv_sem, **device):
    return pltpu.make_async_remote_copy(
        src_ref=src,
        dst_ref=dst,
        send_sem=send_sem,
        recv_sem=recv_sem,
        device_id=device,
        device_id_type=MESH,
    )


def blocks_of(total, width):
    return [(at, min(width, total - at)) for at in range(0, total, width)]


def kernel(
    n_ep,
    n_dp,
    scale,
    ids_ref,
    m1_ref,
    m2_ref,
    x_hbm,
    g_hbm,
    wg_hbm,
    wu_hbm,
    wd_hbm,
    proj_hbm,
    rows_ref,
    first_ref,
    second_ref,
    step_gate_ref,
    step_up_ref,
    step_down_ref,
    x_in,
    g_in,
    wg,
    wu,
    wd,
    proj,
    x_send,
    g_send,
    x_got,
    g_got,
    back_send,
    back_got,
    act_a,
    act_b,
    hidden,
    grads,
    grad_pad,
    chunk_wide,
    part_send,
    part_got,
    sum_send,
    sum_got,
    upd_all,
    upd_pad,
    mom,
    local_sem,
    x_ss,
    x_rs,
    g_ss,
    g_rs,
    b_ss,
    b_rs,
    p_ss,
    p_rs,
    s_ss,
    s_rs,
    u_ss,
    u_rs,
    v_ss,
    v_rs,
):
    ep = lax.axis_index("ep")
    dp = lax.axis_index("dp")
    rows_dev, width = x_in.shape
    ff = wg.shape[1]
    rank = proj.shape[1]
    slots = n_ep * CAP
    n_class = n_dp // GROUP
    per_chunk = 3 * rank // n_dp
    wide = ff // LANES
    chunk_rows = chunk_wide.shape[0] // n_dp
    slab = width // n_dp
    mine_a = dp // GROUP
    mine_b = lax.rem(dp, GROUP)

    loads = [
        pltpu.make_async_copy(x_hbm, x_in, local_sem.at[0]),
        pltpu.make_async_copy(g_hbm, g_in, local_sem.at[1]),
        pltpu.make_async_copy(proj_hbm, proj, local_sem.at[2]),
        pltpu.make_async_copy(wg_hbm, wg, local_sem.at[3]),
        pltpu.make_async_copy(wu_hbm, wu, local_sem.at[4]),
        pltpu.make_async_copy(wd_hbm, wd, local_sem.at[5]),
    ]
    for load in loads:
        load.start()

    barrier = pltpu.get_barrier_semaphore()

    def greet(k, carry):
        pl.semaphore_signal(
            barrier, inc=1, device_id={"ep": lax.rem(ep + k, n_ep)}, device_id_type=MESH
        )
        return carry

    lax.fori_loop(1, n_ep, greet, 0)
    for k in range(1, GROUP):
        peer = mine_a * GROUP + lax.rem(mine_b + k, GROUP)
        pl.semaphore_signal(barrier, inc=1, device_id={"dp": peer}, device_id_type=MESH)
    for k in range(1, n_class):
        peer = lax.rem(mine_a + k, n_class) * GROUP + mine_b
        pl.semaphore_signal(barrier, inc=1, device_id={"dp": peer}, device_id_type=MESH)

    ids = ids_ref[...]
    named = (lax.broadcasted_iota(jnp.int32, (n_ep, rows_dev), 0) == ids).astype(F32)
    before = lax.broadcasted_iota(jnp.int32, (rows_dev, rows_dev), 0) < lax.broadcasted_iota(
        jnp.int32, (rows_dev, rows_dev), 1
    )
    counts = dot(named.astype(BF16), before.astype(F32).astype(BF16))
    ranked = jnp.sum(named * counts, axis=0, keepdims=True)
    place = ids * CAP + ranked.astype(jnp.int32)
    spread32 = (lax.broadcasted_iota(jnp.int32, (slots, rows_dev), 0) == place).astype(F32)
    spread = spread32.astype(BF16)
    gather = spread32.T.astype(BF16)

    def scatter(source, target):
        for at, size in blocks_of(width, 512):
            block = dot(spread, source[:, at : at + size])
            target[:, :, at : at + size] = block.reshape(n_ep, CAP, size).astype(BF16)

    def send_all(source, target, send_sems, recv_sems):
        pltpu.make_async_copy(source.at[ep], target.at[0], recv_sems.at[0]).start()

        def one(k, carry):
            to = lax.rem(ep + k, n_ep)
            remote(
                source.at[to], target.at[k], send_sems.at[k], recv_sems.at[k], ep=to
            ).start()
            return carry

        lax.fori_loop(1, n_ep, one, 0)

    def wait_all(source, target, send_sems, recv_sems):
        pltpu.make_async_copy(source.at[ep], target.at[0], recv_sems.at[0]).wait()

        def one(k, carry):
            to = lax.rem(ep + k, n_ep)
            remote(
                source.at[to], target.at[k], send_sems.at[k], recv_sems.at[k], ep=to
            ).wait_recv()
            return carry

        lax.fori_loop(1, n_ep, one, 0)

    loads[0].wait()
    scatter(x_in, x_send)
    pl.semaphore_wait(barrier, (n_ep - 1) + (GROUP - 1) + (n_class - 1))
    send_all(x_send, x_got, x_ss, x_rs)
    loads[1].wait()
    scatter(g_in, g_send)
    send_all(g_send, g_got, g_ss, g_rs)

    def owner_of(position):
        return lax.rem(position, n_class) * GROUP + position // n_class

    pad_row = lax.broadcasted_iota(jnp.int32, (8 * n_dp, 3 * rank), 0)
    pad_col = lax.broadcasted_iota(jnp.int32, (8 * n_dp, 3 * rank), 1)
    within = lax.rem(pad_row, 8)
    pick = (pad_col == owner_of(pad_row // 8) * per_chunk + within) & (within < per_chunk)
    pick = pick.astype(F32).astype(BF16)
    sel_row = lax.broadcasted_iota(jnp.int32, (3 * rank, 8 * n_dp), 0)
    sel_col = lax.broadcasted_iota(jnp.int32, (3 * rank, 8 * n_dp), 1)
    within = lax.rem(sel_col, 8)
    place_back = (sel_row == owner_of(sel_col // 8) * per_chunk + within) & (within < per_chunk)
    place_back = place_back.astype(F32).astype(BF16)
    loads[2].wait()
    lane_at = pl.multiple_of((dp * slab) // LANES * LANES, LANES)
    part_at = lax.rem(dp * slab, LANES) // slab
    steps_lhs = []
    for kind in range(3):
        piece = proj[min(kind, 2) // 2, :, pl.ds(lane_at, LANES)]
        both = dot_tn(piece, place_back[kind * rank : (kind + 1) * rank])
        chosen = both[0:slab]
        for other in range(1, LANES // slab):
            chosen = jnp.where(part_at == other, both[other * slab : (other + 1) * slab], chosen)
        steps_lhs.append(chosen.astype(BF16))
    steps_lhs = jnp.concatenate(steps_lhs, axis=0)
    mom[...] = jnp.zeros_like(mom)
    for o in range(per_chunk):
        for l in range(wide):
            lanes = slice(o * ff + l * LANES, o * ff + (l + 1) * LANES)
            row = l * per_chunk + o
            mom[0, row : row + 1, :] = m1_ref[:, lanes]
            mom[1, row : row + 1, :] = m2_ref[:, lanes]

    loads[3].wait()
    loads[4].wait()
    loads[5].wait()
    wait_all(x_send, x_got, x_ss, x_rs)
    got = x_got[...].reshape(slots, width)
    for at, size in blocks_of(ff, 256):
        gate_pre = dot(got, wg[:, at : at + size])
        up_pre = dot(got, wu[:, at : at + size])
        sigmoid = 1.0 / (1.0 + jnp.exp(-gate_pre))
        gated = gate_pre * sigmoid
        hidden[:, at : at + size] = (gated * up_pre).astype(BF16)
        act_a[:, at : at + size] = up_pre * sigmoid * (1.0 + gate_pre * (1.0 - sigmoid))
        act_b[:, at : at + size] = gated
    proj_in = dot_nt(proj[0], got)

    def halves(value):
        high = value.astype(BF16)
        return jnp.concatenate([high, (value - high.astype(F32)).astype(BF16)], axis=0)

    proj_in = halves(proj_in)

    wait_all(g_send, g_got, g_ss, g_rs)
    got = g_got[...].reshape(slots, width)
    for at, size in blocks_of(ff, 256):
        hidden_grad = dot_nt(got, wd[at : at + size, :])
        grads[:, at : at + size] = (hidden_grad * act_a[:, at : at + size]).astype(BF16)
        grads[:, ff + at : ff + at + size] = (hidden_grad * act_b[:, at : at + size]).astype(BF16)
    proj_down = halves(dot_nt(proj[1], got))
    terms = []
    for left, right in (
        (proj_in, grads[:, 0:ff]),
        (proj_in, grads[:, ff : 2 * ff]),
        (proj_down, hidden[...]),
    ):
        both = dot(left, right)
        terms.append(((both[0:rank] + both[rank : 2 * rank]) * scale).astype(BF16))
    grad_pad[...] = dot(pick, jnp.concatenate(terms, axis=0))
    for j in range(n_dp):
        for l in range(wide):
            at = j * chunk_rows + l * per_chunk
            chunk_wide[at : at + 8, :] = grad_pad[
                8 * j : 8 * j + 8, l * LANES : (l + 1) * LANES
            ]
    part_send[...] = chunk_wide[...].reshape(n_dp, chunk_rows, LANES).astype(BF16)

    part_copies = []
    for k in range(1, GROUP):
        to = lax.rem(mine_b + k, GROUP)
        part_copies.append(
            remote(
                part_send.at[pl.ds(to * n_class, n_class)],
                part_got.at[k - 1],
                p_ss.at[k],
                p_rs.at[k],
                dp=mine_a * GROUP + to,
            )
        )
    for copy in part_copies:
        copy.start()

    for at, size in blocks_of(width, 256):
        total = dot_nt(grads[:, 0:ff], wg[at : at + size, :]) + dot_nt(
            grads[:, ff : 2 * ff], wu[at : at + size, :]
        )
        back_send[:, :, at : at + size] = total.reshape(n_ep, CAP, size).astype(BF16)
    pltpu.make_async_copy(back_send.at[0], back_got.at[ep], b_rs.at[0]).start()

    def back_copy(k):
        to = lax.rem(ep + n_ep - k, n_ep)
        return remote(back_send.at[k], back_got.at[ep], b_ss.at[k], b_rs.at[k], ep=to)

    def back_start(k, carry):
        back_copy(k).start()
        return carry

    lax.fori_loop(1, n_ep, back_start, 0)

    for copy in part_copies:
        copy.wait_recv()
    total = part_send[pl.ds(mine_b * n_class, n_class)].astype(F32)
    for k in range(1, GROUP):
        total = total + part_got[k - 1].astype(F32)
    sum_send[...] = total.astype(BF16)
    sum_copies = []
    for k in range(1, n_class):
        to = lax.rem(mine_a + k, n_class)
        sum_copies.append(
            remote(
                sum_send.at[to], sum_got.at[k - 1], s_ss.at[k], s_rs.at[k], dp=to * GROUP + mine_b
            )
        )
    for copy in sum_copies:
        copy.start()
    for copy in sum_copies:
        copy.wait_recv()
    grad = sum_send[mine_a].astype(F32)
    for k in range(1, n_class):
        grad = grad + sum_got[k - 1].astype(F32)

    first_new = beta_one * mom[0] + (1.0 - beta_one) * grad
    second_new = beta_two * mom[1] + (1.0 - beta_two) * grad * grad
    update = first_new / bias_one / (jnp.sqrt(second_new / bias_two) + adam_eps)
    my_place = mine_b * n_class + mine_a
    upd_all[my_place] = update.astype(BF16)

    upd_copies = []
    for k in range(1, n_class):
        to = lax.rem(mine_a + k, n_class)
        upd_copies.append(
            remote(
                upd_all.at[my_place],
                upd_all.at[my_place],
                u_ss.at[k],
                u_rs.at[k],
                dp=to * GROUP + mine_b,
            )
        )
    for copy in upd_copies:
        copy.start()

    mom[0] = first_new
    mom[1] = second_new
    for o in range(per_chunk):
        for l in range(wide):
            lanes = slice(o * ff + l * LANES, o * ff + (l + 1) * LANES)
            row = l * per_chunk + o
            first_ref[:, lanes] = mom[0, row : row + 1, :]
            second_ref[:, lanes] = mom[1, row : row + 1, :]

    for k in range(1, n_class):
        source = lax.rem(mine_a + n_class - k, n_class)
        spot = mine_b * n_class + source
        remote(
            upd_all.at[spot], upd_all.at[spot], u_ss.at[k], u_rs.at[k], dp=source * GROUP + mine_b
        ).wait_recv()
    class_copies = []
    for k in range(1, GROUP):
        to = lax.rem(mine_b + k, GROUP)
        span = pl.ds(mine_b * n_class, n_class)
        class_copies.append(
            remote(
                upd_all.at[span],
                upd_all.at[span],
                v_ss.at[k],
                v_rs.at[k],
                dp=mine_a * GROUP + to,
            )
        )
    for copy in class_copies:
        copy.start()

    def back_wait(k, carry):
        came = lax.rem(ep + k, n_ep)
        remote(
            back_send.at[k], back_got.at[came], b_ss.at[k], b_rs.at[k], ep=came
        ).wait_recv()
        return carry

    pltpu.make_async_copy(back_send.at[0], back_got.at[ep], b_rs.at[0]).wait()
    lax.fori_loop(1, n_ep, back_wait, 0)
    for at, size in blocks_of(width, 512):
        block = back_got[:, :, at : at + size].reshape(slots, size)
        rows_ref[:, at : at + size] = dot(gather, block).astype(BF16)

    for k in range(1, GROUP):
        source = lax.rem(mine_b + GROUP - k, GROUP)
        span = pl.ds(source * n_class, n_class)
        remote(
            upd_all.at[span], upd_all.at[span], v_ss.at[k], v_rs.at[k], dp=mine_a * GROUP + source
        ).wait_recv()
    chunk_wide[...] = upd_all[...].astype(F32).reshape(n_dp * chunk_rows, LANES)
    for j in range(n_dp):
        for l in range(wide):
            at = j * chunk_rows + l * per_chunk
            upd_pad[8 * j : 8 * j + 8, l * LANES : (l + 1) * LANES] = chunk_wide[at : at + 8, :]
    steps = dot(steps_lhs, upd_pad[...].astype(BF16)).astype(BF16)
    step_gate_ref[...] = steps[0:slab]
    step_up_ref[...] = steps[slab : 2 * slab]
    step_down_ref[...] = steps[2 * slab : 3 * slab]

    def sent_wait(k, carry):
        to = lax.rem(ep + k, n_ep)
        remote(x_send.at[to], x_got.at[k], x_ss.at[k], x_rs.at[k], ep=to).wait_send()
        remote(g_send.at[to], g_got.at[k], g_ss.at[k], g_rs.at[k], ep=to).wait_send()
        back_copy(k).wait_send()
        return carry

    lax.fori_loop(1, n_ep, sent_wait, 0)
    for copy in part_copies + sum_copies + upd_copies + class_copies:
        copy.wait_send()


def local(rows_in, grads_in, expert_ids, w_gate, w_up, w_down, project, moment_one, moment_two):
    n_ep = lax.axis_size("ep")
    n_dp = lax.axis_size("dp")
    rows_dev, width = rows_in.shape
    ff = w_gate.shape[2]
    rank = project.shape[3]
    slots = n_ep * CAP
    share = moment_one.shape[1]
    chunk_rows = -(-share // (LANES * 16)) * 16
    n_class = n_dp // GROUP
    slab = width // n_dp
    scale = 1.0 / math.sqrt(rows_dev * n_ep * n_dp)
    vmem = pl.BlockSpec(memory_space=pltpu.VMEM)
    anywhere = pl.BlockSpec(memory_space=pl.ANY)
    dma = pltpu.SemaphoreType.DMA
    outs = pl.pallas_call(
        functools.partial(kernel, n_ep, n_dp, scale),
        out_shape=(
            jax.ShapeDtypeStruct((rows_dev, width), BF16),
            jax.ShapeDtypeStruct((1, share), F32),
            jax.ShapeDtypeStruct((1, share), F32),
            jax.ShapeDtypeStruct((slab, ff), BF16),
            jax.ShapeDtypeStruct((slab, ff), BF16),
            jax.ShapeDtypeStruct((slab, ff), BF16),
        ),
        in_specs=[vmem] * 3 + [anywhere] * 6,
        out_specs=(vmem,) * 6,
        scratch_shapes=[
            pltpu.VMEM((rows_dev, width), BF16),
            pltpu.VMEM((rows_dev, width), BF16),
            pltpu.VMEM((width, ff), BF16),
            pltpu.VMEM((width, ff), BF16),
            pltpu.VMEM((ff, width), BF16),
            pltpu.VMEM((2, rank, width), BF16),
            *[pltpu.VMEM((n_ep, CAP, width), BF16)] * 6,
            pltpu.VMEM((slots, ff), F32),
            pltpu.VMEM((slots, ff), F32),
            pltpu.VMEM((slots, ff), BF16),
            pltpu.VMEM((slots, 2 * ff), BF16),
            pltpu.VMEM((8 * n_dp, ff), F32),
            pltpu.VMEM((n_dp * chunk_rows, LANES), F32),
            pltpu.VMEM((n_dp, chunk_rows, LANES), BF16),
            pltpu.VMEM((GROUP - 1, n_class, chunk_rows, LANES), BF16),
            pltpu.VMEM((n_class, chunk_rows, LANES), BF16),
            pltpu.VMEM((n_class - 1, chunk_rows, LANES), BF16),
            pltpu.VMEM((n_dp, chunk_rows, LANES), BF16),
            pltpu.VMEM((8 * n_dp, ff), F32),
            pltpu.VMEM((2, chunk_rows, LANES), F32),
            dma((6,)),
            *[dma((n_ep,))] * 6,
            *[dma((GROUP,))] * 2,
            *[dma((n_class,))] * 4,
            *[dma((GROUP,))] * 2,
        ],
        compiler_params=pltpu.CompilerParams(
            collective_id=0, has_side_effects=True, vmem_limit_bytes=48 << 20
        ),
        cost_estimate=pl.CostEstimate(
            flops=10 * slots * width * ff,
            bytes_accessed=6 * width * ff + 12 * rows_dev * width,
            transcendentals=slots * ff,
        ),
    )(
        expert_ids.reshape(1, rows_dev),
        moment_one,
        moment_two,
        rows_in,
        grads_in,
        w_gate[0],
        w_up[0],
        w_down[0],
        jnp.swapaxes(project[0], 1, 2),
    )
    rows_out, first_new, second_new, step_gate, step_up, step_down = outs
    return (
        rows_out,
        first_new,
        second_new,
        step_gate[None],
        step_up[None],
        jnp.swapaxes(step_down, 0, 1)[None],
    )


def solution(mesh):
    in_specs = (
        P(("ep", "dp"), None),
        P(("ep", "dp"), None),
        P(("ep", "dp"), None),
        P("ep", None, None),
        P("ep", None, None),
        P("ep", None, None),
        P("ep", None, None, None),
        P("ep", "dp"),
        P("ep", "dp"),
    )
    out_specs = (
        P(("ep", "dp"), None),
        P("ep", "dp"),
        P("ep", "dp"),
        P("ep", "dp", None),
        P("ep", "dp", None),
        P("ep", None, "dp"),
    )
    return jax.shard_map(local, mesh=mesh, in_specs=in_specs, out_specs=out_specs, check_vma=False)
```

```python
import functools
import math

import jax
import jax.numpy as jnp
from jax import lax
from jax.experimental import pallas as pl
from jax.experimental.pallas import tpu as pltpu
from jax.sharding import PartitionSpec as P

beta_one = 0.9
beta_two = 0.999
adam_eps = 1e-08
bias_one = 1.0 - 0.9**10
bias_two = 1.0 - 0.999**10

MESH = pl.DeviceIdType.MESH
CAP = 8
GROUP = 4
LANES = 128
F32 = jnp.float32
BF16 = jnp.bfloat16


def dot(a, b):
    return jnp.dot(a, b, preferred_element_type=F32)


def dot_nt(a, b):
    return lax.dot_general(a, b, (((1,), (1,)), ((), ())), preferred_element_type=F32)


def dot_tn(a, b):
    return lax.dot_general(a, b, (((0,), (0,)), ((), ())), preferred_element_type=F32)


def remote(src, dst, send_sem, recv_sem, **device):
    return pltpu.make_async_remote_copy(
        src_ref=src,
        dst_ref=dst,
        send_sem=send_sem,
        recv_sem=recv_sem,
        device_id=device,
        device_id_type=MESH,
    )


def blocks_of(total, width):
    return [(at, min(width, total - at)) for at in range(0, total, width)]


def kernel(
    n_ep,
    n_dp,
    scale,
    ids_hbm,
    m1_hbm,
    m2_hbm,
    x_hbm,
    g_hbm,
    wg_hbm,
    wu_hbm,
    wd_hbm,
    proj_hbm,
    rows_ref,
    first_ref,
    second_ref,
    upd_all,
    lhs_ref,
    ids_ref,
    m1_ref,
    m2_ref,
    x_in,
    g_in,
    wg,
    wu,
    wd,
    proj,
    x_send,
    g_send,
    x_got,
    g_got,
    back_send,
    back_got,
    act_a,
    act_b,
    hidden,
    grads,
    grad_pad,
    chunk_wide,
    part_send,
    part_got,
    sum_send,
    sum_got,
    mom,
    local_sem,
    x_ss,
    x_rs,
    g_ss,
    g_rs,
    b_ss,
    b_rs,
    p_ss,
    p_rs,
    s_ss,
    s_rs,
    u_ss,
    u_rs,
    v_ss,
    v_rs,
    near,
):
    ep = lax.axis_index("ep")
    dp = lax.axis_index("dp")
    rows_dev, width = x_in.shape
    ff = wg.shape[1]
    rank = proj.shape[1]
    slots = n_ep * CAP
    n_class = n_dp // GROUP
    per_chunk = 3 * rank // n_dp
    wide = ff // LANES
    chunk_rows = chunk_wide.shape[0] // n_dp
    slab = width // n_dp
    mine_a = dp // GROUP
    mine_b = lax.rem(dp, GROUP)

    loads = [
        pltpu.make_async_copy(x_hbm, x_in, local_sem.at[0]),
        pltpu.make_async_copy(g_hbm, g_in, local_sem.at[1]),
        pltpu.make_async_copy(proj_hbm, proj, local_sem.at[2]),
        pltpu.make_async_copy(wg_hbm, wg, local_sem.at[3]),
        pltpu.make_async_copy(wu_hbm, wu, local_sem.at[4]),
        pltpu.make_async_copy(wd_hbm, wd, local_sem.at[5]),
    ]
    small = [
        pltpu.make_async_copy(ids_hbm, ids_ref, local_sem.at[6]),
        pltpu.make_async_copy(m1_hbm, m1_ref, local_sem.at[7]),
        pltpu.make_async_copy(m2_hbm, m2_ref, local_sem.at[8]),
    ]
    for load in small[0:1] + loads + small[1:]:
        load.start()

    barrier = pltpu.get_barrier_semaphore()

    def greet(k, carry):
        pl.semaphore_signal(
            barrier, inc=1, device_id={"ep": lax.rem(ep + k, n_ep)}, device_id_type=MESH
        )
        return carry

    lax.fori_loop(1, n_ep, greet, 0)
    def tell(semaphore, offset):
        pl.semaphore_signal(
            semaphore,
            inc=1,
            device_id={"dp": lax.rem(dp + offset, n_dp)},
            device_id_type=MESH,
        )

    tell(barrier, 1)
    tell(barrier, n_dp - 1)

    small[0].wait()
    ids = ids_ref[...]
    named = (lax.broadcasted_iota(jnp.int32, (n_ep, rows_dev), 0) == ids).astype(F32)
    before = lax.broadcasted_iota(jnp.int32, (rows_dev, rows_dev), 0) < lax.broadcasted_iota(
        jnp.int32, (rows_dev, rows_dev), 1
    )
    counts = dot(named.astype(BF16), before.astype(F32).astype(BF16))
    ranked = jnp.sum(named * counts, axis=0, keepdims=True)
    place = ids * CAP + ranked.astype(jnp.int32)
    spread32 = (lax.broadcasted_iota(jnp.int32, (slots, rows_dev), 0) == place).astype(F32)
    spread = spread32.astype(BF16)
    gather = spread32.T.astype(BF16)

    def scatter(source, target):
        for at, size in blocks_of(width, 512):
            block = dot(spread, source[:, at : at + size])
            target[:, :, at : at + size] = block.reshape(n_ep, CAP, size).astype(BF16)

    def send_all(source, target, send_sems, recv_sems):
        pltpu.make_async_copy(source.at[ep], target.at[0], recv_sems.at[0]).start()

        def one(k, carry):
            to = lax.rem(ep + k, n_ep)
            remote(
                source.at[to], target.at[k], send_sems.at[k], recv_sems.at[k], ep=to
            ).start()
            return carry

        lax.fori_loop(1, n_ep, one, 0)

    def wait_all(source, target, send_sems, recv_sems):
        pltpu.make_async_copy(source.at[ep], target.at[0], recv_sems.at[0]).wait()

        def one(k, carry):
            to = lax.rem(ep + k, n_ep)
            remote(
                source.at[to], target.at[k], send_sems.at[k], recv_sems.at[k], ep=to
            ).wait_recv()
            return carry

        lax.fori_loop(1, n_ep, one, 0)

    loads[0].wait()
    scatter(x_in, x_send)
    pl.semaphore_wait(barrier, (n_ep - 1) + 2)
    rounds = [1 << r for r in range((n_dp // 4).bit_length())]
    tell(near.at[0, 0], rounds[0])
    tell(near.at[0, 1], n_dp - rounds[0])
    send_all(x_send, x_got, x_ss, x_rs)
    loads[1].wait()
    scatter(g_in, g_send)
    send_all(g_send, g_got, g_ss, g_rs)

    def owner_of(position):
        return lax.rem(position, n_class) * GROUP + position // n_class

    pad_row = lax.broadcasted_iota(jnp.int32, (8 * n_dp, 3 * rank), 0)
    pad_col = lax.broadcasted_iota(jnp.int32, (8 * n_dp, 3 * rank), 1)
    within = lax.rem(pad_row, 8)
    pick = (pad_col == owner_of(pad_row // 8) * per_chunk + within) & (within < per_chunk)
    pick = pick.astype(F32).astype(BF16)
    sel_row = lax.broadcasted_iota(jnp.int32, (3 * rank, 8 * n_dp), 0)
    sel_col = lax.broadcasted_iota(jnp.int32, (3 * rank, 8 * n_dp), 1)
    within = lax.rem(sel_col, 8)
    place_back = (sel_row == owner_of(sel_col // 8) * per_chunk + within) & (within < per_chunk)
    place_back = place_back.astype(F32).astype(BF16)
    loads[2].wait()
    lane_at = pl.multiple_of((dp * slab) // LANES * LANES, LANES)
    part_at = lax.rem(dp * slab, LANES) // slab
    steps_lhs = []
    for kind in range(3):
        piece = proj[min(kind, 2) // 2, :, pl.ds(lane_at, LANES)]
        both = dot_tn(piece, place_back[kind * rank : (kind + 1) * rank])
        chosen = both[0:slab]
        for other in range(1, LANES // slab):
            chosen = jnp.where(part_at == other, both[other * slab : (other + 1) * slab], chosen)
        steps_lhs.append(chosen.astype(BF16))
    lhs_ref[...] = jnp.concatenate(steps_lhs, axis=0)
    small[1].wait()
    small[2].wait()
    mom[...] = jnp.zeros_like(mom)
    for o in range(per_chunk):
        for l in range(wide):
            lanes = slice(o * ff + l * LANES, o * ff + (l + 1) * LANES)
            row = l * per_chunk + o
            mom[0, row : row + 1, :] = m1_ref[:, lanes]
            mom[1, row : row + 1, :] = m2_ref[:, lanes]

    for r in range(len(rounds)):
        pl.semaphore_wait(near.at[r, 0], 1)
        pl.semaphore_wait(near.at[r, 1], 1)
        if r + 1 < len(rounds):
            tell(near.at[r + 1, 0], rounds[r + 1])
            tell(near.at[r + 1, 1], n_dp - rounds[r + 1])
    loads[3].wait()
    loads[4].wait()
    loads[5].wait()
    wait_all(x_send, x_got, x_ss, x_rs)
    got = x_got[...].reshape(slots, width)
    for at, size in blocks_of(ff, 256):
        gate_pre = dot(got, wg[:, at : at + size])
        up_pre = dot(got, wu[:, at : at + size])
        sigmoid = 1.0 / (1.0 + jnp.exp(-gate_pre))
        gated = gate_pre * sigmoid
        hidden[:, at : at + size] = (gated * up_pre).astype(BF16)
        act_a[:, at : at + size] = up_pre * sigmoid * (1.0 + gate_pre * (1.0 - sigmoid))
        act_b[:, at : at + size] = gated
    proj_in = dot_nt(proj[0], got)

    def halves(value):
        high = value.astype(BF16)
        return jnp.concatenate([high, (value - high.astype(F32)).astype(BF16)], axis=0)

    proj_in = halves(proj_in)

    wait_all(g_send, g_got, g_ss, g_rs)
    got = g_got[...].reshape(slots, width)
    for at, size in blocks_of(ff, 256):
        hidden_grad = dot_nt(got, wd[at : at + size, :])
        grads[:, at : at + size] = (hidden_grad * act_a[:, at : at + size]).astype(BF16)
        grads[:, ff + at : ff + at + size] = (hidden_grad * act_b[:, at : at + size]).astype(BF16)
    proj_down = halves(dot_nt(proj[1], got))
    terms = []
    for left, right in (
        (proj_in, grads[:, 0:ff]),
        (proj_in, grads[:, ff : 2 * ff]),
        (proj_down, hidden[...]),
    ):
        both = dot(left, right)
        terms.append(((both[0:rank] + both[rank : 2 * rank]) * scale).astype(BF16))
    grad_pad[...] = dot(pick, jnp.concatenate(terms, axis=0))
    for j in range(n_dp):
        for l in range(wide):
            at = j * chunk_rows + l * per_chunk
            chunk_wide[at : at + 8, :] = grad_pad[
                8 * j : 8 * j + 8, l * LANES : (l + 1) * LANES
            ]
    part_send[...] = chunk_wide[...].reshape(n_dp, chunk_rows, LANES).astype(BF16)

    part_copies = []
    for k in range(1, GROUP):
        to = lax.rem(mine_b + k, GROUP)
        part_copies.append(
            remote(
                part_send.at[pl.ds(to * n_class, n_class)],
                part_got.at[k - 1],
                p_ss.at[k],
                p_rs.at[k],
                dp=mine_a * GROUP + to,
            )
        )
    for copy in part_copies:
        copy.start()

    for at, size in blocks_of(width, 256):
        total = dot_nt(grads[:, 0:ff], wg[at : at + size, :]) + dot_nt(
            grads[:, ff : 2 * ff], wu[at : at + size, :]
        )
        back_send[:, :, at : at + size] = total.reshape(n_ep, CAP, size).astype(BF16)
    pltpu.make_async_copy(back_send.at[0], back_got.at[ep], b_rs.at[0]).start()

    def back_copy(k):
        to = lax.rem(ep + n_ep - k, n_ep)
        return remote(back_send.at[k], back_got.at[ep], b_ss.at[k], b_rs.at[k], ep=to)

    def back_start(k, carry):
        back_copy(k).start()
        return carry


    for copy in part_copies:
        copy.wait_recv()
    total = part_send[pl.ds(mine_b * n_class, n_class)].astype(F32)
    for k in range(1, GROUP):
        total = total + part_got[k - 1].astype(F32)
    sum_send[...] = total.astype(BF16)
    sum_copies = []
    for k in range(1, n_class):
        to = lax.rem(mine_a + k, n_class)
        sum_copies.append(
            remote(
                sum_send.at[to], sum_got.at[k - 1], s_ss.at[k], s_rs.at[k], dp=to * GROUP + mine_b
            )
        )
    for copy in sum_copies:
        copy.start()
    lax.fori_loop(1, n_ep, back_start, 0)
    for copy in sum_copies:
        copy.wait_recv()
    grad = sum_send[mine_a].astype(F32)
    for k in range(1, n_class):
        grad = grad + sum_got[k - 1].astype(F32)

    first_new = beta_one * mom[0] + (1.0 - beta_one) * grad
    second_new = beta_two * mom[1] + (1.0 - beta_two) * grad * grad
    update = first_new / bias_one / (jnp.sqrt(second_new / bias_two) + adam_eps)
    my_place = mine_b * n_class + mine_a
    upd_all[my_place] = update.astype(BF16)

    upd_copies = []
    for k in range(1, n_class):
        to = lax.rem(mine_a + k, n_class)
        upd_copies.append(
            remote(
                upd_all.at[my_place],
                upd_all.at[my_place],
                u_ss.at[k],
                u_rs.at[k],
                dp=to * GROUP + mine_b,
            )
        )
    for copy in upd_copies:
        copy.start()

    mom[0] = first_new
    mom[1] = second_new
    for o in range(per_chunk):
        for l in range(wide):
            lanes = slice(o * ff + l * LANES, o * ff + (l + 1) * LANES)
            row = l * per_chunk + o
            first_ref[:, lanes] = mom[0, row : row + 1, :]
            second_ref[:, lanes] = mom[1, row : row + 1, :]

    for k in range(1, n_class):
        source = lax.rem(mine_a + n_class - k, n_class)
        spot = mine_b * n_class + source
        remote(
            upd_all.at[spot], upd_all.at[spot], u_ss.at[k], u_rs.at[k], dp=source * GROUP + mine_b
        ).wait_recv()
    class_copies = []
    for k in range(1, GROUP):
        to = lax.rem(mine_b + k, GROUP)
        span = pl.ds(mine_b * n_class, n_class)
        class_copies.append(
            remote(
                upd_all.at[span],
                upd_all.at[span],
                v_ss.at[k],
                v_rs.at[k],
                dp=mine_a * GROUP + to,
            )
        )
    for copy in class_copies:
        copy.start()

    def back_wait(k, carry):
        came = lax.rem(ep + k, n_ep)
        remote(
            back_send.at[k], back_got.at[came], b_ss.at[k], b_rs.at[k], ep=came
        ).wait_recv()
        return carry

    pltpu.make_async_copy(back_send.at[0], back_got.at[ep], b_rs.at[0]).wait()
    lax.fori_loop(1, n_ep, back_wait, 0)
    for at, size in blocks_of(width, 512):
        block = back_got[:, :, at : at + size].reshape(slots, size)
        rows_ref[:, at : at + size] = dot(gather, block).astype(BF16)

    for k in range(1, GROUP):
        source = lax.rem(mine_b + GROUP - k, GROUP)
        span = pl.ds(source * n_class, n_class)
        remote(
            upd_all.at[span], upd_all.at[span], v_ss.at[k], v_rs.at[k], dp=mine_a * GROUP + source
        ).wait_recv()
    def sent_wait(k, carry):
        to = lax.rem(ep + k, n_ep)
        remote(x_send.at[to], x_got.at[k], x_ss.at[k], x_rs.at[k], ep=to).wait_send()
        remote(g_send.at[to], g_got.at[k], g_ss.at[k], g_rs.at[k], ep=to).wait_send()
        back_copy(k).wait_send()
        return carry

    lax.fori_loop(1, n_ep, sent_wait, 0)
    for copy in part_copies + sum_copies + upd_copies + class_copies:
        copy.wait_send()


def finish(n_dp, per_chunk, rows_in, first_in, second_in, upd_in, lhs_in, *refs):
    rows_out, first_out, second_out, step_gate, step_up, step_down = refs[0:6]
    upd_all, lhs, rows, first, second, wide_upd, upd_pad, steps, in_sem, out_sem = refs[6:]
    fetch = [
        pltpu.make_async_copy(source, target, in_sem.at[n])
        for n, (source, target) in enumerate(
            (
                (upd_in, upd_all),
                (lhs_in, lhs),
                (rows_in, rows),
                (first_in, first),
                (second_in, second),
            )
        )
    ]
    for copy in fetch:
        copy.start()
    early = [
        pltpu.make_async_copy(rows, rows_out, out_sem.at[0]),
        pltpu.make_async_copy(first, first_out, out_sem.at[1]),
        pltpu.make_async_copy(second, second_out, out_sem.at[2]),
    ]
    fetch[0].wait()
    fetch[1].wait()
    chunk_rows = upd_all.shape[1]
    ff = upd_pad.shape[1]
    slab = step_gate.shape[0]
    wide_upd[...] = upd_all[...].astype(F32).reshape(n_dp * chunk_rows, LANES)
    for j in range(n_dp):
        for l in range(ff // LANES):
            at = j * chunk_rows + l * per_chunk
            upd_pad[8 * j : 8 * j + 8, l * LANES : (l + 1) * LANES] = wide_upd[at : at + 8, :]
    for copy in fetch[2:]:
        copy.wait()
    for copy in early:
        copy.start()
    late = []
    steps[...] = dot(lhs[...], upd_pad[...].astype(BF16)).reshape(3, slab, ff).astype(BF16)
    for kind, out in enumerate((step_gate, step_up, step_down)):
        late.append(pltpu.make_async_copy(steps.at[kind], out, out_sem.at[3 + kind]))
    for copy in late:
        copy.start()
    for copy in early + late:
        copy.wait()


def local(rows_in, grads_in, expert_ids, w_gate, w_up, w_down, project, moment_one, moment_two):
    n_ep = lax.axis_size("ep")
    n_dp = lax.axis_size("dp")
    rows_dev, width = rows_in.shape
    ff = w_gate.shape[2]
    rank = project.shape[3]
    slots = n_ep * CAP
    share = moment_one.shape[1]
    chunk_rows = -(-share // (LANES * 16)) * 16
    n_class = n_dp // GROUP
    slab = width // n_dp
    scale = 1.0 / math.sqrt(rows_dev * n_ep * n_dp)
    vmem = pl.BlockSpec(memory_space=pltpu.VMEM)
    hbm = pl.BlockSpec(memory_space=pltpu.HBM)
    dma = pltpu.SemaphoreType.DMA
    outs = pl.pallas_call(
        functools.partial(kernel, n_ep, n_dp, scale),
        out_shape=(
            jax.ShapeDtypeStruct((rows_dev, width), BF16),
            jax.ShapeDtypeStruct((1, share), F32),
            jax.ShapeDtypeStruct((1, share), F32),
            jax.ShapeDtypeStruct((n_dp, chunk_rows, LANES), BF16),
            jax.ShapeDtypeStruct((3 * slab, 8 * n_dp), BF16),
        ),
        in_specs=[hbm] * 9,
        out_specs=(vmem,) * 5,
        scratch_shapes=[
            pltpu.VMEM((1, rows_dev), jnp.int32),
            pltpu.VMEM((1, share), F32),
            pltpu.VMEM((1, share), F32),
            pltpu.VMEM((rows_dev, width), BF16),
            pltpu.VMEM((rows_dev, width), BF16),
            pltpu.VMEM((width, ff), BF16),
            pltpu.VMEM((width, ff), BF16),
            pltpu.VMEM((ff, width), BF16),
            pltpu.VMEM((2, rank, width), BF16),
            *[pltpu.VMEM((n_ep, CAP, width), BF16)] * 6,
            pltpu.VMEM((slots, ff), F32),
            pltpu.VMEM((slots, ff), F32),
            pltpu.VMEM((slots, ff), BF16),
            pltpu.VMEM((slots, 2 * ff), BF16),
            pltpu.VMEM((8 * n_dp, ff), F32),
            pltpu.VMEM((n_dp * chunk_rows, LANES), F32),
            pltpu.VMEM((n_dp, chunk_rows, LANES), BF16),
            pltpu.VMEM((GROUP - 1, n_class, chunk_rows, LANES), BF16),
            pltpu.VMEM((n_class, chunk_rows, LANES), BF16),
            pltpu.VMEM((n_class - 1, chunk_rows, LANES), BF16),
            pltpu.VMEM((2, chunk_rows, LANES), F32),
            dma((9,)),
            *[dma((n_ep,))] * 6,
            *[dma((GROUP,))] * 2,
            *[dma((n_class,))] * 4,
            *[dma((GROUP,))] * 2,
            pltpu.SemaphoreType.REGULAR((max(1, n_dp.bit_length() - 2), 2)),
        ],
        compiler_params=pltpu.CompilerParams(
            collective_id=0, has_side_effects=True, vmem_limit_bytes=60 << 20
        ),
        cost_estimate=pl.CostEstimate(
            flops=10 * slots * width * ff,
            bytes_accessed=6 * width * ff + 12 * rows_dev * width,
            transcendentals=slots * ff,
        ),
    )(
        expert_ids.reshape(1, rows_dev),
        moment_one,
        moment_two,
        rows_in,
        grads_in,
        w_gate[0],
        w_up[0],
        w_down[0],
        jnp.swapaxes(project[0], 1, 2),
    )
    rows_out, first_new, second_new, step_gate, step_up, step_down = pl.pallas_call(
        functools.partial(finish, n_dp, 3 * rank // n_dp),
        out_shape=(
            jax.ShapeDtypeStruct((rows_dev, width), BF16),
            jax.ShapeDtypeStruct((1, share), F32),
            jax.ShapeDtypeStruct((1, share), F32),
            jax.ShapeDtypeStruct((slab, ff), BF16),
            jax.ShapeDtypeStruct((slab, ff), BF16),
            jax.ShapeDtypeStruct((slab, ff), BF16),
        ),
        in_specs=[hbm] * 5,
        out_specs=(hbm,) * 6,
        scratch_shapes=[
            pltpu.VMEM((n_dp, chunk_rows, LANES), BF16),
            pltpu.VMEM((3 * slab, 8 * n_dp), BF16),
            pltpu.VMEM((rows_dev, width), BF16),
            pltpu.VMEM((1, share), F32),
            pltpu.VMEM((1, share), F32),
            pltpu.VMEM((n_dp * chunk_rows, LANES), F32),
            pltpu.VMEM((8 * n_dp, ff), F32),
            pltpu.VMEM((3, slab, ff), BF16),
            dma((5,)),
            dma((6,)),
        ],
        compiler_params=pltpu.CompilerParams(vmem_limit_bytes=60 << 20),
    )(*outs)
    return (
        rows_out,
        first_new,
        second_new,
        step_gate[None],
        step_up[None],
        jnp.swapaxes(step_down, 0, 1)[None],
    )


def solution(mesh):
    in_specs = (
        P(("ep", "dp"), None),
        P(("ep", "dp"), None),
        P(("ep", "dp"), None),
        P("ep", None, None),
        P("ep", None, None),
        P("ep", None, None),
        P("ep", None, None, None),
        P("ep", "dp"),
        P("ep", "dp"),
    )
    out_specs = (
        P(("ep", "dp"), None),
        P("ep", "dp"),
        P("ep", "dp"),
        P("ep", "dp", None),
        P("ep", "dp", None),
        P("ep", None, "dp"),
    )
    return jax.shard_map(local, mesh=mesh, in_specs=in_specs, out_specs=out_specs, check_vma=False)
```

```python
import functools
import math

import jax
import jax.numpy as jnp
from jax import lax
from jax.experimental import pallas as pl
from jax.experimental.pallas import tpu as pltpu
from jax.sharding import PartitionSpec as P

beta_one = 0.9
beta_two = 0.999
adam_eps = 1e-08
bias_one = 1.0 - 0.9**10
bias_two = 1.0 - 0.999**10

MESH = pl.DeviceIdType.MESH
CAP = 8
GROUP = 4
LANES = 128
STRIDE = 13
F32 = jnp.float32
BF16 = jnp.bfloat16


def dot(a, b):
    return jnp.dot(a, b, preferred_element_type=F32)


def dot_nt(a, b):
    return lax.dot_general(a, b, (((1,), (1,)), ((), ())), preferred_element_type=F32)


def dot_tn(a, b):
    return lax.dot_general(a, b, (((0,), (0,)), ((), ())), preferred_element_type=F32)


def remote(src, dst, send_sem, recv_sem, **device):
    return pltpu.make_async_remote_copy(
        src_ref=src,
        dst_ref=dst,
        send_sem=send_sem,
        recv_sem=recv_sem,
        device_id=device,
        device_id_type=MESH,
    )


def blocks_of(total, width):
    return [(at, min(width, total - at)) for at in range(0, total, width)]


def kernel(
    n_ep,
    n_dp,
    scale,
    ids_hbm,
    m1_hbm,
    m2_hbm,
    x_hbm,
    g_hbm,
    wg_hbm,
    wu_hbm,
    wd_hbm,
    proj_hbm,
    rows_ref,
    first_ref,
    second_ref,
    upd_all,
    lhs_ref,
    ids_ref,
    m1_ref,
    m2_ref,
    x_in,
    g_in,
    wg,
    wu,
    wd,
    proj,
    x_send,
    g_send,
    x_got,
    g_got,
    back_send,
    back_got,
    act_a,
    act_b,
    hidden,
    grads,
    grad_pad,
    chunk_wide,
    part_send,
    part_got,
    sum_send,
    sum_got,
    mom,
    local_sem,
    x_ss,
    x_rs,
    g_ss,
    g_rs,
    b_ss,
    b_rs,
    p_ss,
    p_rs,
    s_ss,
    s_rs,
    u_ss,
    u_rs,
    v_ss,
    v_rs,
    near,
):
    ep = lax.axis_index("ep")
    dp = lax.axis_index("dp")
    rows_dev, width = x_in.shape
    ff = wg.shape[1]
    rank = proj.shape[1]
    slots = n_ep * CAP
    n_class = n_dp // GROUP
    per_chunk = 3 * rank // n_dp
    wide = ff // LANES
    chunk_rows = chunk_wide.shape[0] // n_dp
    slab = width // n_dp
    mine_a = dp // GROUP
    mine_b = lax.rem(dp, GROUP)

    loads = [
        pltpu.make_async_copy(x_hbm, x_in, local_sem.at[0]),
        pltpu.make_async_copy(g_hbm, g_in, local_sem.at[1]),
        pltpu.make_async_copy(proj_hbm, proj, local_sem.at[2]),
        pltpu.make_async_copy(wg_hbm, wg, local_sem.at[3]),
        pltpu.make_async_copy(wu_hbm, wu, local_sem.at[4]),
        pltpu.make_async_copy(wd_hbm, wd, local_sem.at[5]),
    ]
    small = [
        pltpu.make_async_copy(ids_hbm, ids_ref, local_sem.at[6]),
        pltpu.make_async_copy(m1_hbm, m1_ref, local_sem.at[7]),
        pltpu.make_async_copy(m2_hbm, m2_ref, local_sem.at[8]),
    ]
    for load in small[0:1] + loads + small[1:]:
        load.start()

    barrier = pltpu.get_barrier_semaphore()

    def greet(k, carry):
        pl.semaphore_signal(
            barrier, inc=1, device_id={"ep": lax.rem(ep + k, n_ep)}, device_id_type=MESH
        )
        return carry

    lax.fori_loop(1, n_ep, greet, 0)
    def tell(semaphore, offset):
        pl.semaphore_signal(
            semaphore,
            inc=1,
            device_id={"dp": lax.rem(dp + offset, n_dp)},
            device_id_type=MESH,
        )

    tell(barrier, 1)
    tell(barrier, n_dp - 1)

    small[0].wait()
    ids = ids_ref[...]
    named = (lax.broadcasted_iota(jnp.int32, (n_ep, rows_dev), 0) == ids).astype(F32)
    before = lax.broadcasted_iota(jnp.int32, (rows_dev, rows_dev), 0) < lax.broadcasted_iota(
        jnp.int32, (rows_dev, rows_dev), 1
    )
    counts = dot(named.astype(BF16), before.astype(F32).astype(BF16))
    ranked = jnp.sum(named * counts, axis=0, keepdims=True)
    place = ids * CAP + ranked.astype(jnp.int32)
    spread32 = (lax.broadcasted_iota(jnp.int32, (slots, rows_dev), 0) == place).astype(F32)
    spread = spread32.astype(BF16)
    gather = spread32.T.astype(BF16)

    def scatter(source, target):
        for at, size in blocks_of(width, 512):
            block = dot(spread, source[:, at : at + size])
            target[:, :, at : at + size] = block.reshape(n_ep, CAP, size).astype(BF16)

    def send_all(source, target, send_sems, recv_sems):
        pltpu.make_async_copy(source.at[ep], target.at[0], recv_sems.at[0]).start()

        def one(turn, carry):
            k = lax.rem(turn * STRIDE, n_ep)
            to = lax.rem(ep + k, n_ep)
            remote(
                source.at[to], target.at[k], send_sems.at[k], recv_sems.at[k], ep=to
            ).start()
            return carry

        lax.fori_loop(1, n_ep, one, 0)

    def wait_all(source, target, send_sems, recv_sems):
        pltpu.make_async_copy(source.at[ep], target.at[0], recv_sems.at[0]).wait()

        def one(k, carry):
            to = lax.rem(ep + k, n_ep)
            remote(
                source.at[to], target.at[k], send_sems.at[k], recv_sems.at[k], ep=to
            ).wait_recv()
            return carry

        lax.fori_loop(1, n_ep, one, 0)

    loads[0].wait()
    scatter(x_in, x_send)
    pl.semaphore_wait(barrier, (n_ep - 1) + 2)
    rounds = [1 << r for r in range((n_dp // 4).bit_length())]
    tell(near.at[0, 0], rounds[0])
    tell(near.at[0, 1], n_dp - rounds[0])
    send_all(x_send, x_got, x_ss, x_rs)
    loads[1].wait()
    scatter(g_in, g_send)
    send_all(g_send, g_got, g_ss, g_rs)

    def owner_of(position):
        return lax.rem(position, n_class) * GROUP + position // n_class

    pad_row = lax.broadcasted_iota(jnp.int32, (8 * n_dp, 3 * rank), 0)
    pad_col = lax.broadcasted_iota(jnp.int32, (8 * n_dp, 3 * rank), 1)
    within = lax.rem(pad_row, 8)
    pick = (pad_col == owner_of(pad_row // 8) * per_chunk + within) & (within < per_chunk)
    pick = pick.astype(F32).astype(BF16)
    sel_row = lax.broadcasted_iota(jnp.int32, (3 * rank, 8 * n_dp), 0)
    sel_col = lax.broadcasted_iota(jnp.int32, (3 * rank, 8 * n_dp), 1)
    within = lax.rem(sel_col, 8)
    place_back = (sel_row == owner_of(sel_col // 8) * per_chunk + within) & (within < per_chunk)
    place_back = place_back.astype(F32).astype(BF16)
    loads[2].wait()
    lane_at = pl.multiple_of((dp * slab) // LANES * LANES, LANES)
    part_at = lax.rem(dp * slab, LANES) // slab
    steps_lhs = []
    for kind in range(3):
        piece = proj[min(kind, 2) // 2, :, pl.ds(lane_at, LANES)]
        both = dot_tn(piece, place_back[kind * rank : (kind + 1) * rank])
        chosen = both[0:slab]
        for other in range(1, LANES // slab):
            chosen = jnp.where(part_at == other, both[other * slab : (other + 1) * slab], chosen)
        steps_lhs.append(chosen.astype(BF16))
    lhs_ref[...] = jnp.concatenate(steps_lhs, axis=0)
    small[1].wait()
    small[2].wait()
    mom[...] = jnp.zeros_like(mom)
    for o in range(per_chunk):
        for l in range(wide):
            lanes = slice(o * ff + l * LANES, o * ff + (l + 1) * LANES)
            row = l * per_chunk + o
            mom[0, row : row + 1, :] = m1_ref[:, lanes]
            mom[1, row : row + 1, :] = m2_ref[:, lanes]

    for r in range(len(rounds)):
        pl.semaphore_wait(near.at[r, 0], 1)
        pl.semaphore_wait(near.at[r, 1], 1)
        if r + 1 < len(rounds):
            tell(near.at[r + 1, 0], rounds[r + 1])
            tell(near.at[r + 1, 1], n_dp - rounds[r + 1])
    loads[3].wait()
    loads[4].wait()
    loads[5].wait()
    wait_all(x_send, x_got, x_ss, x_rs)
    got = x_got[...].reshape(slots, width)
    for at, size in blocks_of(ff, 256):
        gate_pre = dot(got, wg[:, at : at + size])
        up_pre = dot(got, wu[:, at : at + size])
        sigmoid = 1.0 / (1.0 + jnp.exp(-gate_pre))
        gated = gate_pre * sigmoid
        hidden[:, at : at + size] = (gated * up_pre).astype(BF16)
        act_a[:, at : at + size] = up_pre * sigmoid * (1.0 + gate_pre * (1.0 - sigmoid))
        act_b[:, at : at + size] = gated
    proj_in = dot_nt(proj[0], got)

    def halves(value):
        high = value.astype(BF16)
        return jnp.concatenate([high, (value - high.astype(F32)).astype(BF16)], axis=0)

    proj_in = halves(proj_in)

    wait_all(g_send, g_got, g_ss, g_rs)
    got = g_got[...].reshape(slots, width)
    for at, size in blocks_of(ff, 256):
        hidden_grad = dot_nt(got, wd[at : at + size, :])
        grads[:, at : at + size] = (hidden_grad * act_a[:, at : at + size]).astype(BF16)
        grads[:, ff + at : ff + at + size] = (hidden_grad * act_b[:, at : at + size]).astype(BF16)
    proj_down = halves(dot_nt(proj[1], got))
    terms = []
    for left, right in (
        (proj_in, grads[:, 0:ff]),
        (proj_in, grads[:, ff : 2 * ff]),
        (proj_down, hidden[...]),
    ):
        both = dot(left, right)
        terms.append(((both[0:rank] + both[rank : 2 * rank]) * scale).astype(BF16))
    grad_pad[...] = dot(pick, jnp.concatenate(terms, axis=0))
    for j in range(n_dp):
        for l in range(wide):
            at = j * chunk_rows + l * per_chunk
            chunk_wide[at : at + 8, :] = grad_pad[
                8 * j : 8 * j + 8, l * LANES : (l + 1) * LANES
            ]
    part_send[...] = chunk_wide[...].reshape(n_dp, chunk_rows, LANES).astype(BF16)

    part_copies = []
    for k in range(1, GROUP):
        to = lax.rem(mine_b + k, GROUP)
        part_copies.append(
            remote(
                part_send.at[pl.ds(to * n_class, n_class)],
                part_got.at[k - 1],
                p_ss.at[k],
                p_rs.at[k],
                dp=mine_a * GROUP + to,
            )
        )
    for copy in part_copies:
        copy.start()

    for at, size in blocks_of(width, 256):
        total = dot_nt(grads[:, 0:ff], wg[at : at + size, :]) + dot_nt(
            grads[:, ff : 2 * ff], wu[at : at + size, :]
        )
        back_send[:, :, at : at + size] = total.reshape(n_ep, CAP, size).astype(BF16)
    pltpu.make_async_copy(back_send.at[0], back_got.at[ep], b_rs.at[0]).start()

    def back_copy(k):
        to = lax.rem(ep + n_ep - k, n_ep)
        return remote(back_send.at[k], back_got.at[ep], b_ss.at[k], b_rs.at[k], ep=to)

    def back_start(turn, carry):
        back_copy(lax.rem(turn * STRIDE, n_ep)).start()
        return carry


    for copy in part_copies:
        copy.wait_recv()
    total = part_send[pl.ds(mine_b * n_class, n_class)].astype(F32)
    for k in range(1, GROUP):
        total = total + part_got[k - 1].astype(F32)
    sum_send[...] = total.astype(BF16)
    sum_copies = []
    for k in range(1, n_class):
        to = lax.rem(mine_a + k, n_class)
        sum_copies.append(
            remote(
                sum_send.at[to], sum_got.at[k - 1], s_ss.at[k], s_rs.at[k], dp=to * GROUP + mine_b
            )
        )
    for copy in sum_copies:
        copy.start()
    lax.fori_loop(1, n_ep, back_start, 0)
    for copy in sum_copies:
        copy.wait_recv()
    grad = sum_send[mine_a].astype(F32)
    for k in range(1, n_class):
        grad = grad + sum_got[k - 1].astype(F32)

    first_new = beta_one * mom[0] + (1.0 - beta_one) * grad
    second_new = beta_two * mom[1] + (1.0 - beta_two) * grad * grad
    update = first_new / bias_one / (jnp.sqrt(second_new / bias_two) + adam_eps)
    my_place = mine_b * n_class + mine_a
    upd_all[my_place] = update.astype(BF16)

    upd_copies = []
    for k in range(1, n_class):
        to = lax.rem(mine_a + k, n_class)
        upd_copies.append(
            remote(
                upd_all.at[my_place],
                upd_all.at[my_place],
                u_ss.at[k],
                u_rs.at[k],
                dp=to * GROUP + mine_b,
            )
        )
    for copy in upd_copies:
        copy.start()

    mom[0] = first_new
    mom[1] = second_new
    for o in range(per_chunk):
        for l in range(wide):
            lanes = slice(o * ff + l * LANES, o * ff + (l + 1) * LANES)
            row = l * per_chunk + o
            first_ref[:, lanes] = mom[0, row : row + 1, :]
            second_ref[:, lanes] = mom[1, row : row + 1, :]

    for k in range(1, n_class):
        source = lax.rem(mine_a + n_class - k, n_class)
        spot = mine_b * n_class + source
        remote(
            upd_all.at[spot], upd_all.at[spot], u_ss.at[k], u_rs.at[k], dp=source * GROUP + mine_b
        ).wait_recv()
    class_copies = []
    for k in range(1, GROUP):
        to = lax.rem(mine_b + k, GROUP)
        span = pl.ds(mine_b * n_class, n_class)
        class_copies.append(
            remote(
                upd_all.at[span],
                upd_all.at[span],
                v_ss.at[k],
                v_rs.at[k],
                dp=mine_a * GROUP + to,
            )
        )
    for copy in class_copies:
        copy.start()

    def back_wait(k, carry):
        came = lax.rem(ep + k, n_ep)
        remote(
            back_send.at[k], back_got.at[came], b_ss.at[k], b_rs.at[k], ep=came
        ).wait_recv()
        return carry

    pltpu.make_async_copy(back_send.at[0], back_got.at[ep], b_rs.at[0]).wait()
    lax.fori_loop(1, n_ep, back_wait, 0)
    for at, size in blocks_of(width, 512):
        block = back_got[:, :, at : at + size].reshape(slots, size)
        rows_ref[:, at : at + size] = dot(gather, block).astype(BF16)

    for k in range(1, GROUP):
        source = lax.rem(mine_b + GROUP - k, GROUP)
        span = pl.ds(source * n_class, n_class)
        remote(
            upd_all.at[span], upd_all.at[span], v_ss.at[k], v_rs.at[k], dp=mine_a * GROUP + source
        ).wait_recv()
    def sent_wait(k, carry):
        to = lax.rem(ep + k, n_ep)
        remote(x_send.at[to], x_got.at[k], x_ss.at[k], x_rs.at[k], ep=to).wait_send()
        remote(g_send.at[to], g_got.at[k], g_ss.at[k], g_rs.at[k], ep=to).wait_send()
        back_copy(k).wait_send()
        return carry

    lax.fori_loop(1, n_ep, sent_wait, 0)
    for copy in part_copies + sum_copies + upd_copies + class_copies:
        copy.wait_send()


def finish(n_dp, per_chunk, rows_in, first_in, second_in, upd_in, lhs_in, *refs):
    rows_out, first_out, second_out, step_gate, step_up, step_down = refs[0:6]
    upd_all, lhs, rows, first, second, wide_upd, upd_pad, steps, in_sem, out_sem = refs[6:]
    fetch = [
        pltpu.make_async_copy(source, target, in_sem.at[n])
        for n, (source, target) in enumerate(
            (
                (upd_in, upd_all),
                (lhs_in, lhs),
                (rows_in, rows),
                (first_in, first),
                (second_in, second),
            )
        )
    ]
    for copy in fetch:
        copy.start()
    early = [
        pltpu.make_async_copy(rows, rows_out, out_sem.at[0]),
        pltpu.make_async_copy(first, first_out, out_sem.at[1]),
        pltpu.make_async_copy(second, second_out, out_sem.at[2]),
    ]
    fetch[0].wait()
    fetch[1].wait()
    chunk_rows = upd_all.shape[1]
    ff = upd_pad.shape[1]
    slab = step_gate.shape[0]
    wide_upd[...] = upd_all[...].astype(F32).reshape(n_dp * chunk_rows, LANES)
    for j in range(n_dp):
        for l in range(ff // LANES):
            at = j * chunk_rows + l * per_chunk
            upd_pad[8 * j : 8 * j + 8, l * LANES : (l + 1) * LANES] = wide_upd[at : at + 8, :]
    for copy in fetch[2:]:
        copy.wait()
    for copy in early:
        copy.start()
    late = []
    steps[...] = dot(lhs[...], upd_pad[...].astype(BF16)).reshape(3, slab, ff).astype(BF16)
    for kind, out in enumerate((step_gate, step_up, step_down)):
        late.append(pltpu.make_async_copy(steps.at[kind], out, out_sem.at[3 + kind]))
    for copy in late:
        copy.start()
    for copy in early + late:
        copy.wait()


def local(rows_in, grads_in, expert_ids, w_gate, w_up, w_down, project, moment_one, moment_two):
    n_ep = lax.axis_size("ep")
    n_dp = lax.axis_size("dp")
    rows_dev, width = rows_in.shape
    ff = w_gate.shape[2]
    rank = project.shape[3]
    slots = n_ep * CAP
    share = moment_one.shape[1]
    chunk_rows = -(-share // (LANES * 16)) * 16
    n_class = n_dp // GROUP
    slab = width // n_dp
    scale = 1.0 / math.sqrt(rows_dev * n_ep * n_dp)
    vmem = pl.BlockSpec(memory_space=pltpu.VMEM)
    hbm = pl.BlockSpec(memory_space=pltpu.HBM)
    dma = pltpu.SemaphoreType.DMA
    outs = pl.pallas_call(
        functools.partial(kernel, n_ep, n_dp, scale),
        out_shape=(
            jax.ShapeDtypeStruct((rows_dev, width), BF16),
            jax.ShapeDtypeStruct((1, share), F32),
            jax.ShapeDtypeStruct((1, share), F32),
            jax.ShapeDtypeStruct((n_dp, chunk_rows, LANES), BF16),
            jax.ShapeDtypeStruct((3 * slab, 8 * n_dp), BF16),
        ),
        in_specs=[hbm] * 9,
        out_specs=(vmem,) * 5,
        scratch_shapes=[
            pltpu.VMEM((1, rows_dev), jnp.int32),
            pltpu.VMEM((1, share), F32),
            pltpu.VMEM((1, share), F32),
            pltpu.VMEM((rows_dev, width), BF16),
            pltpu.VMEM((rows_dev, width), BF16),
            pltpu.VMEM((width, ff), BF16),
            pltpu.VMEM((width, ff), BF16),
            pltpu.VMEM((ff, width), BF16),
            pltpu.VMEM((2, rank, width), BF16),
            *[pltpu.VMEM((n_ep, CAP, width), BF16)] * 6,
            pltpu.VMEM((slots, ff), F32),
            pltpu.VMEM((slots, ff), F32),
            pltpu.VMEM((slots, ff), BF16),
            pltpu.VMEM((slots, 2 * ff), BF16),
            pltpu.VMEM((8 * n_dp, ff), F32),
            pltpu.VMEM((n_dp * chunk_rows, LANES), F32),
            pltpu.VMEM((n_dp, chunk_rows, LANES), BF16),
            pltpu.VMEM((GROUP - 1, n_class, chunk_rows, LANES), BF16),
            pltpu.VMEM((n_class, chunk_rows, LANES), BF16),
            pltpu.VMEM((n_class - 1, chunk_rows, LANES), BF16),
            pltpu.VMEM((2, chunk_rows, LANES), F32),
            dma((9,)),
            *[dma((n_ep,))] * 6,
            *[dma((GROUP,))] * 2,
            *[dma((n_class,))] * 4,
            *[dma((GROUP,))] * 2,
            pltpu.SemaphoreType.REGULAR((max(1, n_dp.bit_length() - 2), 2)),
        ],
        compiler_params=pltpu.CompilerParams(
            collective_id=0, has_side_effects=True, vmem_limit_bytes=60 << 20
        ),
        cost_estimate=pl.CostEstimate(
            flops=10 * slots * width * ff,
            bytes_accessed=6 * width * ff + 12 * rows_dev * width,
            transcendentals=slots * ff,
        ),
    )(
        expert_ids.reshape(1, rows_dev),
        moment_one,
        moment_two,
        rows_in,
        grads_in,
        w_gate[0],
        w_up[0],
        w_down[0],
        jnp.swapaxes(project[0], 1, 2),
    )
    rows_out, first_new, second_new, step_gate, step_up, step_down = pl.pallas_call(
        functools.partial(finish, n_dp, 3 * rank // n_dp),
        out_shape=(
            jax.ShapeDtypeStruct((rows_dev, width), BF16),
            jax.ShapeDtypeStruct((1, share), F32),
            jax.ShapeDtypeStruct((1, share), F32),
            jax.ShapeDtypeStruct((slab, ff), BF16),
            jax.ShapeDtypeStruct((slab, ff), BF16),
            jax.ShapeDtypeStruct((slab, ff), BF16),
        ),
        in_specs=[hbm] * 5,
        out_specs=(hbm,) * 6,
        scratch_shapes=[
            pltpu.VMEM((n_dp, chunk_rows, LANES), BF16),
            pltpu.VMEM((3 * slab, 8 * n_dp), BF16),
            pltpu.VMEM((rows_dev, width), BF16),
            pltpu.VMEM((1, share), F32),
            pltpu.VMEM((1, share), F32),
            pltpu.VMEM((n_dp * chunk_rows, LANES), F32),
            pltpu.VMEM((8 * n_dp, ff), F32),
            pltpu.VMEM((3, slab, ff), BF16),
            dma((5,)),
            dma((6,)),
        ],
        compiler_params=pltpu.CompilerParams(vmem_limit_bytes=60 << 20),
    )(*outs)
    return (
        rows_out,
        first_new,
        second_new,
        step_gate[None],
        step_up[None],
        jnp.swapaxes(step_down, 0, 1)[None],
    )


def solution(mesh):
    in_specs = (
        P(("ep", "dp"), None),
        P(("ep", "dp"), None),
        P(("ep", "dp"), None),
        P("ep", None, None),
        P("ep", None, None),
        P("ep", None, None),
        P("ep", None, None, None),
        P("ep", "dp"),
        P("ep", "dp"),
    )
    out_specs = (
        P(("ep", "dp"), None),
        P("ep", "dp"),
        P("ep", "dp"),
        P("ep", "dp", None),
        P("ep", "dp", None),
        P("ep", None, "dp"),
    )
    return jax.shard_map(local, mesh=mesh, in_specs=in_specs, out_specs=out_specs, check_vma=False)
```
